512 devices in a mesh: row: 32 (over y, x), col: 16 (over z, core).
Axes of the slice: x: 4, y: 8, z: 8, core: 2. Of those that a mesh axis runs over, the one named last changes fastest.
Arguments:
- snapshots: float32 [32768, 8192], P('row', 'col'), may hold values from -400 to 400
Outputs:
- factored: float32 [32768, 8192], P('row', 'col')
- upper: float32 [512, 8192], P(None, 'col')
The draws below stay inside these ranges and needn't reach their ends.
All inputs are finite; a program needn't handle non-finite values.
Results may differ from the reference program's by a relative error of at most 0.00018.
Values sent between devices are 32-bit elements; how exact they have to be, the bound alone decides.
No kernel may reach another device: no remote copies, remote signals or barrier semaphores. Data moves between devices by JAX's collectives and lax.ppermute only.
A program may use at most 64 MiB of HBM per device.

```python
import math
import jax
import jax.numpy as jnp
from jax import lax

R_DEV = 1024
NC = 8192
NB = 256
N_ROW = 32
N_COL = 16


def draw_snapshots(key, part):
    key = jax.random.fold_in(key, 11)
    keys = jax.random.split(key, 5)
    total_rows = R_DEV * N_ROW
    col_dev = NC // N_COL
    latent = jax.random.truncated_normal(keys[0], -6.0, 6.0, (total_rows, 2 * NB), jnp.float32)
    noise = jax.random.truncated_normal(keys[1], -6.0, 6.0, (total_rows, NC), jnp.float32)
    colscale = jnp.exp(jax.random.uniform(keys[2], (NC,), jnp.float32, 0.0, math.log(3.0)))
    rowscale = jnp.exp(jax.random.uniform(keys[3], (total_rows,), jnp.float32, 0.0, math.log(2.0)))
    mixing = jax.random.uniform(keys[4], (NC,), jnp.float32, 0.5, 2.0)
    base = noise + mixing[None, :] * jnp.tile(latent, (1, NC // (2 * NB)))
    panels = latent + 0.6 * jnp.roll(latent, -1, axis=1)
    base = base.at[:, 0:NB].set(panels[:, 0:NB])
    base = base.at[:, col_dev:col_dev + NB].set(panels[:, NB:2 * NB])
    return base * colscale[None, :] * rowscale[:, None]


def setup_inputs(seed: int = 0) -> dict:
    key_of = jax.random.split(jax.random.key(seed), 2)
    snapshots = draw_snapshots(jax.random.fold_in(key_of[1], 71), 0)
    return dict(snapshots=snapshots)


HIGH = lax.Precision.HIGHEST

def reference(snapshots):
    total_rows = snapshots.shape[0]
    col_dev = NC // N_COL
    current = snapshots
    bases = []
    couplings = []
    for start in (0, col_dev):
        panel = current[:, start:start + NB]
        gram = jnp.dot(panel.T.astype(jnp.float32), panel.astype(jnp.float32), precision=HIGH, preferred_element_type=jnp.float32) / total_rows
        lower = jnp.linalg.cholesky(gram)
        basis = lax.linalg.triangular_solve(lower, panel, left_side=False, lower=True, transpose_a=True)
        coupling = jnp.dot(basis.T.astype(jnp.float32), current.astype(jnp.float32), precision=HIGH, preferred_element_type=jnp.float32) / total_rows
        current = current - jnp.dot(basis.astype(jnp.float32), coupling.astype(jnp.float32), precision=HIGH, preferred_element_type=jnp.float32)
        bases.append(basis)
        couplings.append(coupling)
    factored = current.at[:, 0:NB].set(bases[0]).at[:, col_dev:col_dev + NB].set(bases[1])
    upper = jnp.concatenate(couplings, axis=0)
    return (factored, upper)
```

```python
import jax
import jax.numpy as jnp
from jax import lax
from jax.experimental import pallas as pl
from jax.experimental.pallas import tpu as pltpu
from jax.sharding import PartitionSpec as P

NB = 256
BLK = 128


def lane(x, c):
    return jnp.broadcast_to(x[:, c:c + 1], (8, BLK))

def sub(x, j):
    return jnp.broadcast_to(x[j:j + 1, :], (8, BLK))

def eliminate(s, w):
    n = len(s)
    for g in range(n):
        c0 = 8 * g
        v = [lane(s[g], c0 + j) for j in range(8)]
        p = {(i, j): sub(v[j], i) for j in range(8) for i in range(j + 1)}
        r = [None] * 8
        u = {}
        hs, hw = [None] * 8, [None] * 8
        for j in range(8):
            d = p[j, j]
            r[j] = lax.rsqrt(d)
            for k in range(j + 1, 8):
                u[j, k] = p[j, k] * r[j]
            for a in range(j + 1, 8):
                for b in range(a, 8):
                    p[a, b] = p[a, b] - u[j, a] * u[j, b]
        for j in range(8):
            a, b = sub(s[g], j), sub(w[g], j)
            for m in range(j):
                a = a - u[m, j] * hs[m]
                b = b - u[m, j] * hw[m]
            hs[j], hw[j] = a * r[j], b * r[j]
        for i in range(g + 1, n):
            f = []
            for j in range(8):
                t = lane(s[i], c0 + j)
                for m in range(j):
                    t = t - f[m] * u[m, j]
                f.append(t * r[j])
            for j in range(8):
                s[i] = s[i] - f[j] * hs[j]
                w[i] = w[i] - f[j] * hw[j]
        row = lax.broadcasted_iota(jnp.int32, (8, BLK), 0)
        a, b = hs[0], hw[0]
        for j in range(1, 8):
            a = jnp.where(row == j, hs[j], a)
            b = jnp.where(row == j, hw[j], b)
        s[g], w[g] = a, b
    return s, w

def dot(a, b, dims):
    return lax.dot_general(a, b, (dims, ((), ())), precision=lax.Precision.HIGHEST, preferred_element_type=jnp.float32)

def invert(s_ref, x_ref):
    n = s_ref.shape[0]
    nb = n // BLK
    row = lax.broadcasted_iota(jnp.int32, (n, n), 0)
    col = lax.broadcasted_iota(jnp.int32, (n, n), 1)
    x_ref[...] = jnp.where(row == col, 1.0, 0.0).astype(jnp.float32)
    for k in range(nb):
        lo, hi = k * BLK, (k + 1) * BLK
        r8 = lax.broadcasted_iota(jnp.int32, (8, BLK), 0)
        c8 = lax.broadcasted_iota(jnp.int32, (8, BLK), 1)
        s = [s_ref[lo + 8 * i:lo + 8 * i + 8, lo:hi] for i in range(16)]
        w = [jnp.where(c8 == r8 + 8 * i, 1.0, 0.0).astype(jnp.float32) for i in range(16)]
        s, w = eliminate(s, w)
        inv = jnp.concatenate(w, axis=0)
        x_ref[lo:hi, lo:hi] = inv
        if k:
            x_ref[lo:hi, :lo] = dot(inv, x_ref[lo:hi, :lo], ((1,), (0,)))
        if k + 1 < nb:
            right = dot(inv, s_ref[lo:hi, hi:], ((1,), (0,)))
            s_ref[hi:, hi:] = s_ref[hi:, hi:] - dot(right, right, ((0,), (0,)))
            x_ref[hi:, :hi] = x_ref[hi:, :hi] - dot(right, x_ref[lo:hi, :hi], ((0,), (0,)))


def split(value):
    high = value.astype(jnp.bfloat16)
    return high, (value - high.astype(jnp.float32)).astype(jnp.bfloat16)


def dot3(left, right, dims):
    (a, b), (c, d) = left, right
    out = None
    for x, y in ((b, c), (a, d), (a, c)):
        term = lax.dot_general(x, y, (dims, ((), ())), preferred_element_type=jnp.float32)
        out = term if out is None else out + term
    return out


NN, NT, TN = ((1,), (0,)), ((1,), (1,)), ((0,), (0,))


def unfold(part):
    wide, rest = part[:32], part[32:]
    left = jnp.concatenate([wide[:, :NB], wide[:, NB:]], axis=0)
    right = jnp.concatenate([rest[:, BLK * i:BLK * i + BLK] for i in range(4)], axis=0)
    return left, right


def factor_kernel(core_ref, gram_ref, pair_ref, panel_ref, other_ref, inverse_ref, basis_ref, s_ref):
    even = core_ref[0] == 0
    nx = gram_ref.shape[0]
    for x in range(nx):
        rows = slice(x * 64, x * 64 + 64)
        left, right = unfold(gram_ref[x])
        left2, right2 = unfold(pair_ref[x])
        s_ref[rows, :NB] = jnp.where(even, left, left2)
        s_ref[rows, NB:NB + BLK] = jnp.where(even, right, right2)
        s_ref[rows, NB + BLK:] = jnp.where(even, right2, right)
        s_ref[NB + x * 64:NB + x * 64 + 64, NB:] = jnp.where(even, left2, left)
    invert(s_ref, inverse_ref)
    x11 = split(inverse_ref[:NB, :NB])
    x21 = split(inverse_ref[NB:, :NB])
    x22 = split(inverse_ref[NB:, NB:])

    def tile(i, carry):
        rows = pl.ds(pl.multiple_of(i * 256, 256), 256)
        mine, other = panel_ref[rows, :], other_ref[rows, :]
        one, two = split(jnp.where(even, mine, other)), split(jnp.where(even, other, mine))
        basis_ref[rows, :NB] = dot3(one, x11, NT)
        basis_ref[rows, NB:] = dot3(one, x21, NT) + dot3(two, x22, NT)
        return carry

    lax.fori_loop(0, panel_ref.shape[0] // 256, tile, 0)


def finish_kernel(column_ref, snap_ref, basis_ref, inverse_ref, inner_ref, out_ref, upper_ref, c_ref):
    column = column_ref[0]
    ny, nx, cut, _ = inner_ref.shape
    shift = (column % 2) * NB
    for x in range(nx):
        for y in range(ny):
            at = lax.rem(x * ny * cut + y * cut + shift, 2 * NB)
            c_ref[pl.ds(pl.multiple_of(at, cut), cut), :] = inner_ref[y, x]
    c1, c2 = split(c_ref[:NB, :]), split(c_ref[NB:, :])
    k1 = dot3(split(inverse_ref[:NB, :NB]), c1, NN)
    k2 = dot3(split(inverse_ref[NB:, :NB]), c1, NN) + dot3(split(inverse_ref[NB:, NB:]), c2, NN)
    upper_ref[:NB, :] = k1
    upper_ref[NB:, :] = k2
    k1, k2 = split(k1), split(k2)

    def tile(i, carry):
        rows = pl.ds(pl.multiple_of(i * 256, 256), 256)
        one, two = basis_ref[rows, :NB], basis_ref[rows, NB:]
        out = snap_ref[rows, :] - (dot3(split(one), k1, NN) + dot3(split(two), k2, NN))
        out_ref[rows, NB:] = out[:, NB:]
        own = jnp.where(column == 0, one, two)
        out_ref[rows, :NB] = jnp.where(column < 2, own, out[:, :NB])
        return carry

    lax.fori_loop(0, snap_ref.shape[0] // 256, tile, 0)


SMEM, VMEM = pl.BlockSpec(memory_space=pltpu.SMEM), pl.BlockSpec(memory_space=pltpu.VMEM)


def call(kernel, shapes, scratch, flops, *operands):
    return pl.pallas_call(
        kernel,
        out_shape=[jax.ShapeDtypeStruct(s, jnp.float32) for s in shapes],
        in_specs=[SMEM] + [VMEM] * (len(operands) - 1),
        out_specs=[VMEM] * len(shapes),
        scratch_shapes=[pltpu.VMEM(scratch, jnp.float32)],
        compiler_params=pltpu.CompilerParams(vmem_limit_bytes=48 << 20),
        cost_estimate=pl.CostEstimate(flops=flops, bytes_accessed=8 << 20, transcendentals=0),
    )(*operands)


def product(left, right, dims, precision):
    return lax.dot_general(
        left, right, (dims, ((), ())), precision=precision, preferred_element_type=jnp.float32
    )


HIGHEST, HIGH = lax.Precision.HIGHEST, lax.Precision.HIGH
NX = 4


def trade(parts, axis, groups):
    return lax.all_to_all(parts, axis, 0, 0, axis_index_groups=groups)


def copies(part, n):
    return jnp.broadcast_to(part[None], (n, *part.shape))


def fold(part):
    wide = jnp.concatenate([part[:, :32, :NB], part[:, 32:, :NB]], axis=2)
    rest = jnp.concatenate([part[:, 16 * i:16 * i + 16, NB:] for i in range(4)], axis=2)
    return jnp.concatenate([wide, rest], axis=1)


def body(snapshots):
    n_row, n_col = lax.axis_size("row"), lax.axis_size("col")
    nx, ny, nz = NX, n_row // NX, n_col // 2
    x_groups = [[y * nx + x for x in range(nx)] for y in range(ny)]
    y_groups = [[y * nx + x for y in range(ny)] for x in range(nx)]
    z_groups = [[2 * z + c for z in range(nz)] for c in range(2)]
    swap = [(i, i ^ 1) for i in range(n_col)]

    rows, width = snapshots.shape
    scale = 1.0 / (rows * n_row)
    column = lax.axis_index("col")
    core, z = column % 2, column // 2
    even = core == 0

    mine = snapshots[:, :NB]
    step = rows // nz
    piece = jnp.where(z == 0, mine[:step], 0.0)
    for k in range(1, nz):
        piece = piece + lax.ppermute(
            mine[k * step:(k + 1) * step], "col", [(c, 2 * k + c) for c in range(2)]
        )
    panel = trade(copies(piece, nz), "col", z_groups).reshape(rows, NB)

    other = lax.ppermute(panel, "col", swap)

    inner = jnp.concatenate(
        [product(panel, snapshots, TN, HIGH), product(other, snapshots, TN, HIGH)], axis=0
    )
    first = jnp.where(even, panel, other)
    second = jnp.where(even, other[:, :BLK], panel[:, BLK:])
    gram = jnp.concatenate(
        [product(panel, panel, TN, HIGHEST), product(first, second, TN, HIGHEST)], axis=1
    )
    cut = 2 * NB // nx
    gram = fold(gram.reshape(nx, NB // nx, 3 * BLK))
    inner = jnp.concatenate([inner.reshape(nx, cut, width), gram], axis=1)
    sums = jnp.sum(trade(inner, "row", x_groups), axis=0) * scale
    inner = sums[:cut].reshape(ny, cut // ny, width)
    gram = copies(sums[cut:], ny)
    sums = jnp.sum(trade(jnp.concatenate([inner, gram], axis=1), "row", y_groups), axis=0)
    cut //= ny
    parts = trade(copies(sums, nx), "row", x_groups)
    inner = trade(copies(parts[:, :cut].reshape(nx * cut, width), ny), "row", y_groups)
    gram = parts[:, cut:]

    inverse, basis = call(
        factor_kernel,
        [(2 * NB, 2 * NB), (rows, 2 * NB)],
        (2 * NB, 2 * NB),
        20 << 30,
        core.astype(jnp.int32).reshape(1), gram, lax.ppermute(gram, "col", swap), panel, other,
    )
    factored, upper = call(
        finish_kernel,
        [(rows, width), (2 * NB, width)],
        (2 * NB, width),
        4 << 30,
        column.astype(jnp.int32).reshape(1), snapshots, basis, inverse,
        inner.reshape(ny, nx, cut, width),
    )
    return (factored, upper)


def solution(mesh):
    return jax.shard_map(
        body,
        mesh=mesh,
        in_specs=(P("row", "col"),),
        out_specs=(P("row", "col"), P(None, "col")),
        check_vma=False,
    )
```

```python
import jax
import jax.numpy as jnp
from jax import lax
from jax.experimental import pallas as pl
from jax.experimental.pallas import tpu as pltpu
from jax.sharding import PartitionSpec as P

NB = 256
BLK = 128


def lane(x, c):
    return jnp.broadcast_to(x[:, c:c + 1], (8, BLK))

def sub(x, j):
    return jnp.broadcast_to(x[j:j + 1, :], (8, BLK))

def eliminate(s, w):
    n = len(s)
    for g in range(n):
        c0 = 8 * g
        v = [lane(s[g], c0 + j) for j in range(8)]
        p = {(i, j): sub(v[j], i) for j in range(8) for i in range(j + 1)}
        r = [None] * 8
        u = {}
        hs, hw = [None] * 8, [None] * 8
        for j in range(8):
            d = p[j, j]
            r[j] = lax.rsqrt(d)
            for k in range(j + 1, 8):
                u[j, k] = p[j, k] * r[j]
            for a in range(j + 1, 8):
                for b in range(a, 8):
                    p[a, b] = p[a, b] - u[j, a] * u[j, b]
        for j in range(8):
            a, b = sub(s[g], j), sub(w[g], j)
            for m in range(j):
                a = a - u[m, j] * hs[m]
                b = b - u[m, j] * hw[m]
            hs[j], hw[j] = a * r[j], b * r[j]
        for i in range(g + 1, n):
            f = []
            for j in range(8):
                t = lane(s[i], c0 + j)
                for m in range(j):
                    t = t - f[m] * u[m, j]
                f.append(t * r[j])
            for j in range(8):
                s[i] = s[i] - f[j] * hs[j]
                w[i] = w[i] - f[j] * hw[j]
        row = lax.broadcasted_iota(jnp.int32, (8, BLK), 0)
        a, b = hs[0], hw[0]
        for j in range(1, 8):
            a = jnp.where(row == j, hs[j], a)
            b = jnp.where(row == j, hw[j], b)
        s[g], w[g] = a, b
    return s, w

def dot(a, b, dims):
    return lax.dot_general(a, b, (dims, ((), ())), precision=lax.Precision.HIGHEST, preferred_element_type=jnp.float32)

def invert(s_ref, x_ref):
    n = s_ref.shape[0]
    nb = n // BLK
    row = lax.broadcasted_iota(jnp.int32, (n, n), 0)
    col = lax.broadcasted_iota(jnp.int32, (n, n), 1)
    x_ref[...] = jnp.where(row == col, 1.0, 0.0).astype(jnp.float32)
    for k in range(nb):
        lo, hi = k * BLK, (k + 1) * BLK
        r8 = lax.broadcasted_iota(jnp.int32, (8, BLK), 0)
        c8 = lax.broadcasted_iota(jnp.int32, (8, BLK), 1)
        s = [s_ref[lo + 8 * i:lo + 8 * i + 8, lo:hi] for i in range(16)]
        w = [jnp.where(c8 == r8 + 8 * i, 1.0, 0.0).astype(jnp.float32) for i in range(16)]
        s, w = eliminate(s, w)
        inv = jnp.concatenate(w, axis=0)
        x_ref[lo:hi, lo:hi] = inv
        if k:
            x_ref[lo:hi, :lo] = dot(inv, x_ref[lo:hi, :lo], ((1,), (0,)))
        if k + 1 < nb:
            right = dot(inv, s_ref[lo:hi, hi:], ((1,), (0,)))
            s_ref[hi:, hi:] = s_ref[hi:, hi:] - dot(right, right, ((0,), (0,)))
            x_ref[hi:, :hi] = x_ref[hi:, :hi] - dot(right, x_ref[lo:hi, :hi], ((0,), (0,)))


def split(value):
    high = value.astype(jnp.bfloat16)
    return high, (value - high.astype(jnp.float32)).astype(jnp.bfloat16)


def dot3(left, right, dims):
    (a, b), (c, d) = left, right
    out = None
    for x, y in ((b, c), (a, d), (a, c)):
        term = lax.dot_general(x, y, (dims, ((), ())), preferred_element_type=jnp.float32)
        out = term if out is None else out + term
    return out


NN, NT, TN = ((1,), (0,)), ((1,), (1,)), ((0,), (0,))


def inner_kernel(column_ref, snap_ref, panel_ref, other_ref, out_ref, gram_ref):
    column = column_ref[0]
    even, z = column % 2 == 0, column // 2
    nx, tall, width = out_ref.shape
    cut = 2 * NB // nx
    mine, other = panel_ref[...], other_ref[...]
    snap = split(snap_ref[...])
    for k, part in enumerate((mine, other)):
        inner = dot3(split(part), snap, TN)
        for x in range(nx // 2):
            out_ref[k * nx // 2 + x, :cut, :] = inner[x * cut:x * cut + cut]
    first = jnp.where(even, mine, other)
    second = jnp.where(even, other[:, :BLK], mine[:, BLK:])
    gram_ref[:, :NB], gram_ref[:, NB:] = dot(mine, mine, TN), dot(first, second, TN)
    for x in range(nx):
        rows = pl.ds(pl.multiple_of(x * (NB // nx) + z * 8, 8), 8)
        out_ref[x, cut:cut + 8, :3 * BLK] = gram_ref[rows, :]
        out_ref[x, cut:cut + 8, 3 * BLK:] = jnp.zeros((8, width - 3 * BLK), jnp.float32)
        out_ref[x, cut + 8:, :] = jnp.zeros((tall - cut - 8, width), jnp.float32)


def factor_kernel(core_ref, gram_ref, pair_ref, inverse_ref, s_ref):
    even = core_ref[0] == 0
    nx = gram_ref.shape[0]
    for x in range(nx):
        rows = slice(x * 64, x * 64 + 64)
        left, right = gram_ref[x, :, :NB], gram_ref[x, :, NB:3 * BLK]
        left2, right2 = pair_ref[x, :, :NB], pair_ref[x, :, NB:3 * BLK]
        s_ref[rows, :NB] = jnp.where(even, left, left2)
        s_ref[rows, NB:NB + BLK] = jnp.where(even, right, right2)
        s_ref[rows, NB + BLK:] = jnp.where(even, right2, right)
        s_ref[NB + x * 64:NB + x * 64 + 64, NB:] = jnp.where(even, left2, left)
    invert(s_ref, inverse_ref)


def finish_kernel(
    column_ref, snap_ref, panel_ref, other_ref, inverse_ref, inner_ref, out_ref, upper_ref, c_ref, half_ref
):
    column = column_ref[0]
    even = column % 2 == 0
    ny, nx, cut, _ = inner_ref.shape
    blocks = ((slice(0, NB), slice(0, NB)), (slice(NB, 2 * NB), slice(0, NB)), (slice(NB, 2 * NB), slice(NB, 2 * NB)))

    @pl.when(pl.program_id(0) == 0)
    def _():
        shift = (column % 2) * NB
        for x in range(nx):
            for y in range(ny):
                at = lax.rem(x * ny * cut + y * cut + shift, 2 * NB)
                c_ref[pl.ds(pl.multiple_of(at, cut), cut), :] = inner_ref[y, x]
        x11, x21, x22 = (split(inverse_ref[b]) for b in blocks)
        c1, c2 = split(c_ref[:NB, :]), split(c_ref[NB:, :])
        k1 = dot3(x11, c1, NN)
        k2 = dot3(x21, c1, NN) + dot3(x22, c2, NN)
        upper_ref[:NB, :] = k1
        upper_ref[NB:, :] = k2
        for i, part in enumerate((x11, x21, x22)):
            half_ref[2 * i], half_ref[2 * i + 1] = part[0], part[1]
        for i, k in enumerate((k1, k2)):
            for j, part in enumerate(split(k)):
                half_ref[6 + 2 * i + j], half_ref[10 + 2 * i + j] = part[:, :NB], part[:, NB:]

    x11, x21, x22 = ((half_ref[2 * i], half_ref[2 * i + 1]) for i in range(3))
    mine, other = panel_ref[...], other_ref[...]
    one, two = split(jnp.where(even, mine, other)), split(jnp.where(even, other, mine))
    one, two = dot3(one, x11, NT), dot3(one, x21, NT) + dot3(two, x22, NT)
    own = jnp.where(column == 0, one, two)
    one, two = split(one), split(two)
    for h in range(2):
        at = slice(h * NB, h * NB + NB)
        k1, k2 = ((half_ref[6 + 4 * h + 2 * i], half_ref[7 + 4 * h + 2 * i]) for i in range(2))
        out = snap_ref[:, at] - (dot3(one, k1, NN) + dot3(two, k2, NN))
        out_ref[:, at] = jnp.where(column < 2, own, out) if h == 0 else out


SMEM, VMEM = pl.BlockSpec(memory_space=pltpu.SMEM), pl.BlockSpec(memory_space=pltpu.VMEM)


def call(kernel, shapes, scratch, flops, *operands):
    return pl.pallas_call(
        kernel,
        out_shape=[jax.ShapeDtypeStruct(s, jnp.float32) for s in shapes],
        in_specs=[SMEM] + [VMEM] * (len(operands) - 1),
        out_specs=[VMEM] * len(shapes),
        scratch_shapes=[pltpu.VMEM(s, jnp.float32) for s in scratch],
        compiler_params=pltpu.CompilerParams(vmem_limit_bytes=24 << 20),
        cost_estimate=pl.CostEstimate(flops=flops, bytes_accessed=8 << 20, transcendentals=0),
    )(*operands)


def finish(column, snapshots, panel, other, inverse, inner):
    rows, width = snapshots.shape
    tile = 256

    def whole(shape):
        return pl.BlockSpec(shape, lambda i: (0,) * len(shape))

    def tiles(columns):
        return pl.BlockSpec((tile, columns), lambda i: (i, 0))

    return pl.pallas_call(
        finish_kernel,
        grid=(rows // tile,),
        out_shape=[
            jax.ShapeDtypeStruct((rows, width), jnp.float32),
            jax.ShapeDtypeStruct((2 * NB, width), jnp.float32),
        ],
        in_specs=[SMEM, tiles(width), tiles(NB), tiles(NB), whole(inverse.shape), whole(inner.shape)],
        out_specs=[tiles(width), whole((2 * NB, width))],
        scratch_shapes=[
            pltpu.VMEM((2 * NB, width), jnp.float32), pltpu.VMEM((14, NB, NB), jnp.bfloat16)
        ],
        compiler_params=pltpu.CompilerParams(vmem_limit_bytes=60 << 20),
        cost_estimate=pl.CostEstimate(flops=4 << 30, bytes_accessed=8 << 20, transcendentals=0),
    )(column, snapshots, panel, other, inverse, inner)


NX = 4


def trade(parts, axis, groups):
    return lax.all_to_all(parts, axis, 0, 0, axis_index_groups=groups)


def copies(part, n):
    return jnp.broadcast_to(part[None], (n, *part.shape))


def body(snapshots):
    n_row, n_col = lax.axis_size("row"), lax.axis_size("col")
    nx, ny, nz = NX, n_row // NX, n_col // 2
    x_groups = [[y * nx + x for x in range(nx)] for y in range(ny)]
    y_groups = [[y * nx + x for y in range(ny)] for x in range(nx)]
    z_groups = [[2 * z + c for z in range(nz)] for c in range(2)]
    swap = [(i, i ^ 1) for i in range(n_col)]

    rows, width = snapshots.shape
    scale = 1.0 / (rows * n_row)
    column = lax.axis_index("col")
    z = column // 2

    mine = snapshots[:, :NB]
    step = rows // nz
    piece = jnp.where(z == 0, mine[:step], 0.0)
    for k in range(1, nz):
        piece = piece + lax.ppermute(
            mine[k * step:(k + 1) * step], "col", [(c, 2 * k + c) for c in range(2)]
        )
    panel = trade(copies(piece, nz), "col", z_groups).reshape(rows, NB)

    other = lax.ppermute(panel, "col", swap)

    place = column.astype(jnp.int32).reshape(1)
    cut = 2 * NB // nx
    inner, = call(
        inner_kernel, [(nx, cut + 16, width)], [(NB, 3 * BLK)], 4 << 30, place, snapshots, panel, other
    )
    sums = jnp.sum(trade(inner, "row", x_groups), axis=0) * scale
    inner = sums[:cut].reshape(ny, cut // ny, width)
    gram = copies(sums[cut:cut + 8], ny)
    cut //= ny
    sums = jnp.sum(trade(jnp.concatenate([inner, gram], axis=1), "row", y_groups), axis=0)
    gram = trade(copies(sums[cut:], nz), "col", z_groups).reshape(8 * nz, width)
    parts = trade(copies(jnp.concatenate([sums[:cut], gram], axis=0), nx), "row", x_groups)
    inner = trade(copies(parts[:, :cut].reshape(nx * cut, width), ny), "row", y_groups)
    gram = parts[:, cut:]

    inverse, = call(
        factor_kernel,
        [(2 * NB, 2 * NB)],
        [(2 * NB, 2 * NB)],
        20 << 30,
        place % 2, gram, lax.ppermute(gram, "col", swap),
    )
    factored, upper = finish(
        place, snapshots, panel, other, inverse,
        inner.reshape(ny, nx, cut, width),
    )
    return (factored, upper)


def solution(mesh):
    return jax.shard_map(
        body,
        mesh=mesh,
        in_specs=(P("row", "col"),),
        out_specs=(P("row", "col"), P(None, "col")),
        check_vma=False,
    )
```

```python
import jax
import jax.numpy as jnp
from jax import lax
from jax.experimental import pallas as pl
from jax.experimental.pallas import tpu as pltpu
from jax.sharding import PartitionSpec as P

NB = 256
BLK = 128


def lane(x, c):
    return jnp.broadcast_to(x[:, c:c + 1], (8, BLK))

def sub(x, j):
    return jnp.broadcast_to(x[j:j + 1, :], (8, BLK))

def eliminate(s, w):
    n = len(s)
    for g in range(n):
        c0 = 8 * g
        v = [lane(s[g], c0 + j) for j in range(8)]
        p = {(i, j): sub(v[j], i) for j in range(8) for i in range(j + 1)}
        r = [None] * 8
        u = {}
        hs, hw = [None] * 8, [None] * 8
        for j in range(8):
            d = p[j, j]
            r[j] = lax.rsqrt(d)
            for k in range(j + 1, 8):
                u[j, k] = p[j, k] * r[j]
            for a in range(j + 1, 8):
                for b in range(a, 8):
                    p[a, b] = p[a, b] - u[j, a] * u[j, b]
        for j in range(8):
            a, b = sub(s[g], j), sub(w[g], j)
            for m in range(j):
                a = a - u[m, j] * hs[m]
                b = b - u[m, j] * hw[m]
            hs[j], hw[j] = a * r[j], b * r[j]
        for i in range(g + 1, n):
            f = []
            for j in range(8):
                t = lane(s[i], c0 + j)
                for m in range(j):
                    t = t - f[m] * u[m, j]
                f.append(t * r[j])
            for j in range(8):
                s[i] = s[i] - f[j] * hs[j]
                w[i] = w[i] - f[j] * hw[j]
        row = lax.broadcasted_iota(jnp.int32, (8, BLK), 0)
        a, b = hs[0], hw[0]
        for j in range(1, 8):
            a = jnp.where(row == j, hs[j], a)
            b = jnp.where(row == j, hw[j], b)
        s[g], w[g] = a, b
    return s, w

def dot(a, b, dims):
    return lax.dot_general(a, b, (dims, ((), ())), precision=lax.Precision.HIGHEST, preferred_element_type=jnp.float32)

def invert(s_ref, x_ref):
    n = s_ref.shape[0]
    nb = n // BLK
    row = lax.broadcasted_iota(jnp.int32, (n, n), 0)
    col = lax.broadcasted_iota(jnp.int32, (n, n), 1)
    x_ref[...] = jnp.where(row == col, 1.0, 0.0).astype(jnp.float32)
    for k in range(nb):
        lo, hi = k * BLK, (k + 1) * BLK
        r8 = lax.broadcasted_iota(jnp.int32, (8, BLK), 0)
        c8 = lax.broadcasted_iota(jnp.int32, (8, BLK), 1)
        s = [s_ref[lo + 8 * i:lo + 8 * i + 8, lo:hi] for i in range(16)]
        w = [jnp.where(c8 == r8 + 8 * i, 1.0, 0.0).astype(jnp.float32) for i in range(16)]
        s, w = eliminate(s, w)
        inv = jnp.concatenate(w, axis=0)
        x_ref[lo:hi, lo:hi] = inv
        if k:
            x_ref[lo:hi, :lo] = dot(inv, x_ref[lo:hi, :lo], ((1,), (0,)))
        if k + 1 < nb:
            right = dot(inv, s_ref[lo:hi, hi:], ((1,), (0,)))
            s_ref[hi:, hi:] = s_ref[hi:, hi:] - dot(right, right, ((0,), (0,)))
            x_ref[hi:, :hi] = x_ref[hi:, :hi] - dot(right, x_ref[lo:hi, :hi], ((0,), (0,)))


def split(value):
    high = value.astype(jnp.bfloat16)
    return high, (value - high.astype(jnp.float32)).astype(jnp.bfloat16)


def dot3(left, right, dims):
    (a, b), (c, d) = left, right
    out = None
    for x, y in ((b, c), (a, d), (a, c)):
        term = lax.dot_general(x, y, (dims, ((), ())), preferred_element_type=jnp.float32)
        out = term if out is None else out + term
    return out


NN, NT, TN = ((1,), (0,)), ((1,), (1,)), ((0,), (0,))


def inner_kernel(column_ref, snap_ref, panel_ref, other_ref, out_ref, gram_ref):
    column = column_ref[0]
    even, z = column % 2 == 0, column // 2
    nx, tall, width = out_ref.shape
    cut = 2 * NB // nx
    mine, other = panel_ref[...], other_ref[...]
    snap = split(snap_ref[...])
    for k, part in enumerate((mine, other)):
        inner = dot3(split(part), snap, TN)
        for x in range(nx // 2):
            out_ref[k * nx // 2 + x, :cut, :] = inner[x * cut:x * cut + cut]
    first = jnp.where(even, mine, other)
    second = jnp.where(even, other[:, :BLK], mine[:, BLK:])
    gram_ref[:, :NB], gram_ref[:, NB:] = dot(mine, mine, TN), dot(first, second, TN)
    for x in range(nx):
        rows = pl.ds(pl.multiple_of(x * (NB // nx) + z * 8, 8), 8)
        out_ref[x, cut:cut + 8, :3 * BLK] = gram_ref[rows, :]
        out_ref[x, cut:cut + 8, 3 * BLK:] = jnp.zeros((8, width - 3 * BLK), jnp.float32)
        out_ref[x, cut + 8:, :] = jnp.zeros((tall - cut - 8, width), jnp.float32)


def factor_kernel(core_ref, gram_ref, pair_ref, inverse_ref, s_ref):
    even = core_ref[0] == 0
    nx = gram_ref.shape[0]
    for x in range(nx):
        rows = slice(x * 64, x * 64 + 64)
        left, right = gram_ref[x, :, :NB], gram_ref[x, :, NB:3 * BLK]
        left2, right2 = pair_ref[x, :, :NB], pair_ref[x, :, NB:3 * BLK]
        s_ref[rows, :NB] = jnp.where(even, left, left2)
        s_ref[rows, NB:NB + BLK] = jnp.where(even, right, right2)
        s_ref[rows, NB + BLK:] = jnp.where(even, right2, right)
        s_ref[NB + x * 64:NB + x * 64 + 64, NB:] = jnp.where(even, left2, left)
    invert(s_ref, inverse_ref)


def finish_kernel(
    column_ref, snap_ref, panel_ref, other_ref, inverse_ref, inner_ref, out_ref, upper_ref, c_ref, half_ref
):
    column = column_ref[0]
    even = column % 2 == 0
    ny, nx, cut, _ = inner_ref.shape
    blocks = ((slice(0, NB), slice(0, NB)), (slice(NB, 2 * NB), slice(0, NB)), (slice(NB, 2 * NB), slice(NB, 2 * NB)))

    @pl.when(pl.program_id(0) == 0)
    def _():
        shift = (column % 2) * NB
        for x in range(nx):
            for y in range(ny):
                at = lax.rem(x * ny * cut + y * cut + shift, 2 * NB)
                c_ref[pl.ds(pl.multiple_of(at, cut), cut), :] = inner_ref[y, x]
        x11, x21, x22 = (split(inverse_ref[b]) for b in blocks)
        c1, c2 = split(c_ref[:NB, :]), split(c_ref[NB:, :])
        k1 = dot3(x11, c1, NN)
        k2 = dot3(x21, c1, NN) + dot3(x22, c2, NN)
        upper_ref[:NB, :] = k1
        upper_ref[NB:, :] = k2
        for i, part in enumerate((x11, x21, x22)):
            half_ref[2 * i], half_ref[2 * i + 1] = part[0], part[1]
        for i, k in enumerate((k1, k2)):
            for j, part in enumerate(split(k)):
                half_ref[6 + 2 * i + j], half_ref[10 + 2 * i + j] = part[:, :NB], part[:, NB:]

    x11, x21, x22 = ((half_ref[2 * i], half_ref[2 * i + 1]) for i in range(3))
    mine, other = panel_ref[...], other_ref[...]
    one, two = split(jnp.where(even, mine, other)), split(jnp.where(even, other, mine))
    one, two = dot3(one, x11, NT), dot3(one, x21, NT) + dot3(two, x22, NT)
    own = jnp.where(column == 0, one, two)
    one, two = split(one), split(two)
    for h in range(2):
        at = slice(h * NB, h * NB + NB)
        k1, k2 = ((half_ref[6 + 4 * h + 2 * i], half_ref[7 + 4 * h + 2 * i]) for i in range(2))
        out = snap_ref[:, at] - (dot3(one, k1, NN) + dot3(two, k2, NN))
        out_ref[:, at] = jnp.where(column < 2, own, out) if h == 0 else out


SMEM, VMEM = pl.BlockSpec(memory_space=pltpu.SMEM), pl.BlockSpec(memory_space=pltpu.VMEM)


def call(kernel, shapes, scratch, flops, *operands):
    return pl.pallas_call(
        kernel,
        out_shape=[jax.ShapeDtypeStruct(s, jnp.float32) for s in shapes],
        in_specs=[SMEM] + [VMEM] * (len(operands) - 1),
        out_specs=[VMEM] * len(shapes),
        scratch_shapes=[pltpu.VMEM(s, jnp.float32) for s in scratch],
        compiler_params=pltpu.CompilerParams(vmem_limit_bytes=24 << 20),
        cost_estimate=pl.CostEstimate(flops=flops, bytes_accessed=8 << 20, transcendentals=0),
    )(*operands)


def finish(column, snapshots, panel, other, inverse, inner):
    rows, width = snapshots.shape
    tile = 256

    def whole(shape):
        return pl.BlockSpec(shape, lambda i: (0,) * len(shape))

    def tiles(columns):
        return pl.BlockSpec((tile, columns), lambda i: (i, 0))

    return pl.pallas_call(
        finish_kernel,
        grid=(rows // tile,),
        out_shape=[
            jax.ShapeDtypeStruct((rows, width), jnp.float32),
            jax.ShapeDtypeStruct((2 * NB, width), jnp.float32),
        ],
        in_specs=[SMEM, tiles(width), tiles(NB), tiles(NB), whole(inverse.shape), whole(inner.shape)],
        out_specs=[tiles(width), whole((2 * NB, width))],
        scratch_shapes=[
            pltpu.VMEM((2 * NB, width), jnp.float32), pltpu.VMEM((14, NB, NB), jnp.bfloat16)
        ],
        compiler_params=pltpu.CompilerParams(vmem_limit_bytes=60 << 20),
        cost_estimate=pl.CostEstimate(flops=4 << 30, bytes_accessed=8 << 20, transcendentals=0),
    )(column, snapshots, panel, other, inverse, inner)


NX = 4


def trade(parts, axis, groups):
    return lax.all_to_all(parts, axis, 0, 0, axis_index_groups=groups)


def copies(part, n):
    return jnp.broadcast_to(part[None], (n, *part.shape))


def body(snapshots):
    n_row, n_col = lax.axis_size("row"), lax.axis_size("col")
    nx, ny, nz = NX, n_row // NX, n_col // 2
    x_groups = [[y * nx + x for x in range(nx)] for y in range(ny)]
    y_groups = [[y * nx + x for y in range(ny)] for x in range(nx)]
    z_groups = [[2 * z + c for z in range(nz)] for c in range(2)]
    swap = [(i, i ^ 1) for i in range(n_col)]

    rows, width = snapshots.shape
    scale = 1.0 / (rows * n_row)
    column = lax.axis_index("col")
    z = column // 2

    mine = snapshots[:, :NB]
    step = rows // nz
    piece = jnp.where(z == 0, mine[:step], 0.0)
    for k in range(1, nz):
        piece = piece + lax.ppermute(
            mine[k * step:(k + 1) * step], "col", [(c, 2 * k + c) for c in range(2)]
        )
    panel = trade(copies(piece, nz), "col", z_groups).reshape(rows, NB)

    other = lax.ppermute(panel, "col", swap)

    place = column.astype(jnp.int32).reshape(1)
    cut = 2 * NB // nx
    inner, = call(
        inner_kernel, [(nx, cut + 16, width)], [(NB, 3 * BLK)], 4 << 30, place, snapshots, panel, other
    )
    sums = jnp.sum(trade(inner, "row", x_groups), axis=0) * scale
    inner = sums[:cut].reshape(ny, cut // ny, width)
    gram = copies(sums[cut:cut + 8], ny)
    cut //= ny
    sums = jnp.sum(trade(jnp.concatenate([inner, gram], axis=1), "row", y_groups), axis=0)
    gram = trade(copies(sums[cut:], nz), "col", z_groups).reshape(8 * nz, width)
    parts = trade(copies(jnp.concatenate([sums[:cut], gram], axis=0), nx), "row", x_groups)
    inner = trade(copies(parts[:, :cut].reshape(nx * cut, width), ny), "row", y_groups)
    gram = parts[:, cut:]

    inverse, = call(
        factor_kernel,
        [(2 * NB, 2 * NB)],
        [(2 * NB, 2 * NB)],
        1 << 30,
        place % 2, gram, lax.ppermute(gram, "col", swap),
    )
    factored, upper = finish(
        place, snapshots, panel, other, inverse,
        inner.reshape(ny, nx, cut, width),
    )
    return (factored, upper)


def solution(mesh):
    return jax.shard_map(
        body,
        mesh=mesh,
        in_specs=(P("row", "col"),),
        out_specs=(P("row", "col"), P(None, "col")),
        check_vma=False,
    )
```

```python
import jax
import jax.numpy as jnp
from jax import lax
from jax.experimental import pallas as pl
from jax.experimental.pallas import tpu as pltpu
from jax.sharding import PartitionSpec as P

NB = 256
BLK = 128


def lane(x, c):
    return jnp.broadcast_to(x[:, c:c + 1], (8, BLK))

def sub(x, j):
    return jnp.broadcast_to(x[j:j + 1, :], (8, BLK))

def eliminate(s, w):
    n = len(s)
    for g in range(n):
        c0 = 8 * g
        v = [lane(s[g], c0 + j) for j in range(8)]
        p = {(i, j): sub(v[j], i) for j in range(8) for i in range(j + 1)}
        r = [None] * 8
        u = {}
        hs, hw = [None] * 8, [None] * 8
        for j in range(8):
            d = p[j, j]
            r[j] = lax.rsqrt(d)
            for k in range(j + 1, 8):
                u[j, k] = p[j, k] * r[j]
            for a in range(j + 1, 8):
                for b in range(a, 8):
                    p[a, b] = p[a, b] - u[j, a] * u[j, b]
        for j in range(8):
            a, b = sub(s[g], j), sub(w[g], j)
            for m in range(j):
                a = a - u[m, j] * hs[m]
                b = b - u[m, j] * hw[m]
            hs[j], hw[j] = a * r[j], b * r[j]
        for i in range(g + 1, n):
            f = []
            for j in range(8):
                t = lane(s[i], c0 + j)
                for m in range(j):
                    t = t - f[m] * u[m, j]
                f.append(t * r[j])
            for j in range(8):
                s[i] = s[i] - f[j] * hs[j]
                w[i] = w[i] - f[j] * hw[j]
        row = lax.broadcasted_iota(jnp.int32, (8, BLK), 0)
        a, b = hs[0], hw[0]
        for j in range(1, 8):
            a = jnp.where(row == j, hs[j], a)
            b = jnp.where(row == j, hw[j], b)
        s[g], w[g] = a, b
    return s, w

def dot(a, b, dims):
    return lax.dot_general(a, b, (dims, ((), ())), precision=lax.Precision.HIGHEST, preferred_element_type=jnp.float32)

def invert(s_ref, x_ref):
    n = s_ref.shape[0]
    nb = n // BLK
    row = lax.broadcasted_iota(jnp.int32, (n, n), 0)
    col = lax.broadcasted_iota(jnp.int32, (n, n), 1)
    x_ref[...] = jnp.where(row == col, 1.0, 0.0).astype(jnp.float32)
    for k in range(nb):
        lo, hi = k * BLK, (k + 1) * BLK
        r8 = lax.broadcasted_iota(jnp.int32, (8, BLK), 0)
        c8 = lax.broadcasted_iota(jnp.int32, (8, BLK), 1)
        s = [s_ref[lo + 8 * i:lo + 8 * i + 8, lo:hi] for i in range(16)]
        w = [jnp.where(c8 == r8 + 8 * i, 1.0, 0.0).astype(jnp.float32) for i in range(16)]
        s, w = eliminate(s, w)
        inv = jnp.concatenate(w, axis=0)
        x_ref[lo:hi, lo:hi] = inv
        if k:
            x_ref[lo:hi, :lo] = dot(inv, x_ref[lo:hi, :lo], ((1,), (0,)))
        if k + 1 < nb:
            right = dot(inv, s_ref[lo:hi, hi:], ((1,), (0,)))
            s_ref[hi:, hi:] = s_ref[hi:, hi:] - dot(right, right, ((0,), (0,)))
            x_ref[hi:, :hi] = x_ref[hi:, :hi] - dot(right, x_ref[lo:hi, :hi], ((0,), (0,)))


def split(value):
    high = value.astype(jnp.bfloat16)
    return high, (value - high.astype(jnp.float32)).astype(jnp.bfloat16)


def dot3(left, right, dims):
    (a, b), (c, d) = left, right
    out = None
    for x, y in ((b, c), (a, d), (a, c)):
        term = lax.dot_general(x, y, (dims, ((), ())), preferred_element_type=jnp.float32)
        out = term if out is None else out + term
    return out


NN, NT, TN = ((1,), (0,)), ((1,), (1,)), ((0,), (0,))


def inner_kernel(column_ref, snap_ref, panel_ref, other_ref, out_ref, gram_ref):
    column = column_ref[0]
    even, z = column % 2 == 0, column // 2
    nx, _, width = out_ref.shape
    cut = 2 * NB // nx
    mine, other = panel_ref[...], other_ref[...]
    snap = split(snap_ref[...])
    for k, part in enumerate((mine, other)):
        inner = dot3(split(part), snap, TN)
        for x in range(nx // 2):
            out_ref[k * nx // 2 + x, :cut, :] = inner[x * cut:x * cut + cut]
    first = jnp.where(even, mine, other)
    second = jnp.where(even, other[:, :BLK], mine[:, BLK:])
    gram_ref[:, :NB], gram_ref[:, NB:] = dot(mine, mine, TN), dot(first, second, TN)
    for x in range(nx):
        rows = pl.ds(pl.multiple_of(x * (NB // nx) + z * 8, 8), 8)
        out_ref[x, cut:cut + 8, :3 * BLK] = gram_ref[rows, :]
        out_ref[x, cut:cut + 8, 3 * BLK:] = jnp.zeros((8, width - 3 * BLK), jnp.float32)


def factor_kernel(core_ref, gram_ref, pair_ref, inverse_ref, s_ref):
    even = core_ref[0] == 0
    nx = gram_ref.shape[0]
    for x in range(nx):
        rows = slice(x * 64, x * 64 + 64)
        left, right = gram_ref[x, :, :NB], gram_ref[x, :, NB:3 * BLK]
        left2, right2 = pair_ref[x, :, :NB], pair_ref[x, :, NB:3 * BLK]
        s_ref[rows, :NB] = jnp.where(even, left, left2)
        s_ref[rows, NB:NB + BLK] = jnp.where(even, right, right2)
        s_ref[rows, NB + BLK:] = jnp.where(even, right2, right)
        s_ref[NB + x * 64:NB + x * 64 + 64, NB:] = jnp.where(even, left2, left)
    invert(s_ref, inverse_ref)


def finish_kernel(
    column_ref, snap_ref, panel_ref, other_ref, inverse_ref, inner_ref, out_ref, upper_ref, c_ref, half_ref
):
    column = column_ref[0]
    even = column % 2 == 0
    ny, nx, cut, _ = inner_ref.shape
    blocks = ((slice(0, NB), slice(0, NB)), (slice(NB, 2 * NB), slice(0, NB)), (slice(NB, 2 * NB), slice(NB, 2 * NB)))

    @pl.when(pl.program_id(0) == 0)
    def _():
        shift = (column % 2) * NB
        for x in range(nx):
            for y in range(ny):
                at = lax.rem(x * ny * cut + y * cut + shift, 2 * NB)
                c_ref[pl.ds(pl.multiple_of(at, cut), cut), :] = inner_ref[y, x]
        x11, x21, x22 = (split(inverse_ref[b]) for b in blocks)
        c1, c2 = split(c_ref[:NB, :]), split(c_ref[NB:, :])
        k1 = dot3(x11, c1, NN)
        k2 = dot3(x21, c1, NN) + dot3(x22, c2, NN)
        upper_ref[:NB, :] = k1
        upper_ref[NB:, :] = k2
        for i, part in enumerate((x11, x21, x22)):
            half_ref[2 * i], half_ref[2 * i + 1] = part[0], part[1]
        for i, k in enumerate((k1, k2)):
            for j, part in enumerate(split(k)):
                half_ref[6 + 2 * i + j], half_ref[10 + 2 * i + j] = part[:, :NB], part[:, NB:]

    x11, x21, x22 = ((half_ref[2 * i], half_ref[2 * i + 1]) for i in range(3))
    mine, other = panel_ref[...], other_ref[...]
    one, two = split(jnp.where(even, mine, other)), split(jnp.where(even, other, mine))
    one, two = dot3(one, x11, NT), dot3(one, x21, NT) + dot3(two, x22, NT)
    own = jnp.where(column == 0, one, two)
    one, two = split(one), split(two)
    for h in range(2):
        at = slice(h * NB, h * NB + NB)
        k1, k2 = ((half_ref[6 + 4 * h + 2 * i], half_ref[7 + 4 * h + 2 * i]) for i in range(2))
        out = snap_ref[:, at] - (dot3(one, k1, NN) + dot3(two, k2, NN))
        out_ref[:, at] = jnp.where(column < 2, own, out) if h == 0 else out


SMEM, VMEM = pl.BlockSpec(memory_space=pltpu.SMEM), pl.BlockSpec(memory_space=pltpu.VMEM)


def call(kernel, shapes, scratch, flops, *operands):
    return pl.pallas_call(
        kernel,
        out_shape=[jax.ShapeDtypeStruct(s, jnp.float32) for s in shapes],
        in_specs=[SMEM] + [VMEM] * (len(operands) - 1),
        out_specs=[VMEM] * len(shapes),
        scratch_shapes=[pltpu.VMEM(s, jnp.float32) for s in scratch],
        compiler_params=pltpu.CompilerParams(vmem_limit_bytes=24 << 20),
        cost_estimate=pl.CostEstimate(flops=flops, bytes_accessed=8 << 20, transcendentals=0),
    )(*operands)


def finish(column, snapshots, panel, other, inverse, inner):
    rows, width = snapshots.shape
    tile = 512

    def whole(shape):
        return pl.BlockSpec(shape, lambda i: (0,) * len(shape))

    def tiles(columns):
        return pl.BlockSpec((tile, columns), lambda i: (i, 0))

    return pl.pallas_call(
        finish_kernel,
        grid=(rows // tile,),
        out_shape=[
            jax.ShapeDtypeStruct((rows, width), jnp.float32),
            jax.ShapeDtypeStruct((2 * NB, width), jnp.float32),
        ],
        in_specs=[SMEM, tiles(width), tiles(NB), tiles(NB), whole(inverse.shape), whole(inner.shape)],
        out_specs=[tiles(width), whole((2 * NB, width))],
        scratch_shapes=[
            pltpu.VMEM((2 * NB, width), jnp.float32), pltpu.VMEM((14, NB, NB), jnp.bfloat16)
        ],
        compiler_params=pltpu.CompilerParams(vmem_limit_bytes=60 << 20),
        cost_estimate=pl.CostEstimate(flops=4 << 30, bytes_accessed=8 << 20, transcendentals=0),
    )(column, snapshots, panel, other, inverse, inner)


NX = 4


def trade(parts, axis, groups):
    return lax.all_to_all(parts, axis, 0, 0, axis_index_groups=groups)


def copies(part, n):
    return jnp.broadcast_to(part[None], (n, *part.shape))


def body(snapshots):
    n_row, n_col = lax.axis_size("row"), lax.axis_size("col")
    nx, ny, nz = NX, n_row // NX, n_col // 2
    x_groups = [[y * nx + x for x in range(nx)] for y in range(ny)]
    y_groups = [[y * nx + x for y in range(ny)] for x in range(nx)]
    z_groups = [[2 * z + c for z in range(nz)] for c in range(2)]
    swap = [(i, i ^ 1) for i in range(n_col)]

    rows, width = snapshots.shape
    scale = 1.0 / (rows * n_row)
    column = lax.axis_index("col")
    z = column // 2

    mine = snapshots[:, :NB]
    step = rows // nz
    piece = jnp.where(z == 0, mine[:step], 0.0)
    for k in range(1, nz):
        piece = piece + lax.ppermute(
            mine[k * step:(k + 1) * step], "col", [(c, 2 * k + c) for c in range(2)]
        )
    panel = trade(copies(piece, nz), "col", z_groups).reshape(rows, NB)

    other = lax.ppermute(panel, "col", swap)

    place = column.astype(jnp.int32).reshape(1)
    cut = 2 * NB // nx
    inner, = call(
        inner_kernel, [(nx, cut + 8, width)], [(NB, 3 * BLK)], 4 << 30, place, snapshots, panel, other
    )
    sums = jnp.sum(trade(inner, "row", x_groups), axis=0) * scale
    inner = sums[:cut].reshape(ny, cut // ny, width)
    gram = copies(sums[cut:cut + 8], ny)
    cut //= ny
    sums = jnp.sum(trade(jnp.concatenate([inner, gram], axis=1), "row", y_groups), axis=0)
    gram = trade(copies(sums[cut:], nz), "col", z_groups).reshape(8 * nz, width)
    parts = trade(copies(jnp.concatenate([sums[:cut], gram], axis=0), nx), "row", x_groups)
    inner = trade(copies(parts[:, :cut].reshape(nx * cut, width), ny), "row", y_groups)
    gram = parts[:, cut:]

    inverse, = call(
        factor_kernel,
        [(2 * NB, 2 * NB)],
        [(2 * NB, 2 * NB)],
        1 << 30,
        place % 2, gram, lax.ppermute(gram, "col", swap),
    )
    factored, upper = finish(
        place, snapshots, panel, other, inverse,
        inner.reshape(ny, nx, cut, width),
    )
    return (factored, upper)


def solution(mesh):
    return jax.shard_map(
        body,
        mesh=mesh,
        in_specs=(P("row", "col"),),
        out_specs=(P("row", "col"), P(None, "col")),
        check_vma=False,
    )
```
